32 devices in a mesh: groups: 2 (over y), expert: 8 (over z, x), tensor: 2 (over core).
Axes of the slice: x: 2, y: 2, z: 4, core: 2. Of those that a mesh axis runs over, the one named last changes fastest.
Arguments:
- tokens: bfloat16 [2048, 7168], P(('groups', 'expert'), 'tensor'), parts along dimension 0, may hold values from -6 to 6
- expert_ids: int32 [2048, 8], P(('groups', 'expert')), parts along dimension 0, may hold values from 0 to 255, all different within a row; in each aligned block of 128 rows (0 to 127, 128 to 255, ...) at most 8 rows name the same one
- route_weight: float32 [2048, 8], P(('groups', 'expert')), parts along dimension 0, may hold values from 0.2 to 1
- gate_weight: bfloat16 [8, 7168, 2048], P('expert', 'tensor'), may hold values from -0.0625 to 0.0625
- up_weight: bfloat16 [8, 7168, 2048], P('expert', 'tensor'), may hold values from -0.0625 to 0.0625
- down_weight: bfloat16 [8, 2048, 7168], P('expert', None, 'tensor'), may hold values from -0.125 to 0.125
Outputs:
- mixed: bfloat16 [2048, 7168], P(('groups', 'expert'), 'tensor'), parts along dimension 0
The draws below stay inside these ranges and needn't reach their ends.
There are 2 independent parts, one for each index of `groups`. The reference program is written for one: setup_inputs(seed, part) draws one part's arguments, and reference() takes and returns one part's arrays. A program takes and returns all parts, laid end to end along the dimension named above; an argument that names none is the same for every part. Nothing has to cross between parts.
Inputs may be any that keep to these rules, and one draw needn't show every extreme that they name: `expert_ids`: each row names 8 different experts; among the rows of one index of expert (128 rows, in order) no expert is named more than 8 times, a bound that some block reaches.
All inputs are finite; a program needn't handle non-finite values.
Results may differ from the reference program's by a relative error of at most 0.0057.
Values may be sent and summed in bfloat16 or wider, within the bound.
No kernel may reach another device: no remote copies, remote signals or barrier semaphores. Data moves between devices by JAX's collectives and lax.ppermute only.
A program may use at most 192 MiB of HBM per device.

```python
import math
import jax
import jax.numpy as jnp
import numpy as np
from jax import lax

D = 7168
HIDDEN_SIZE = 2048
TOP = 8
ROUTED = 256
TOK_DEV = 128
SPLIT = 1
EXPERTS = 8
PIECES = 8
PIECE_H = 2048
TOKENS = 1024
SLOT = 8


def steps_of(rng, dims, pieces, least, high):
    def one(dim, blocks):
        heights = jax.random.uniform(jax.random.fold_in(jax.random.fold_in(rng, 6), dim), (blocks,), jnp.float32, least / len(pieces), high / len(pieces))
        return jnp.repeat(jnp.exp(heights), dims[dim] // blocks).reshape((-1,) + (1,) * (len(dims) - dim - 1))

    loudness = one(*pieces[0])
    for cut in pieces[1:]:
        loudness = loudness * one(*cut)
    return loudness


def shared_out(key, own, number, rows, amount, top, bound, lean):
    ranking = jax.random.permutation(key, amount)
    heavy_load, usual = load_shares(amount, rows * top, bound, lean, True), load_shares(amount, rows * top, bound, lean, False)
    places = jnp.arange(amount)

    def named(tallies, turn):
        used = int((tallies > 0).sum())
        fixed = max(1, used // 4)
        moved = fixed + (places - fixed + turn * (used - fixed)) % max(1, amount - fixed)
        return jnp.zeros((amount,), jnp.int32).at[ranking[jnp.where(places < fixed, places, moved)]].set(jnp.asarray(tallies, jnp.int32))

    tallies = jnp.where(number % 4 == 0, named(heavy_load, number // 4), named(usual, number - number // 4 - 1))
    mixed = jax.random.permutation(jax.random.fold_in(own, 3), amount)
    source_of, sink = mixed[0:amount // 2 * 2:2], mixed[1:amount // 2 * 2:2]
    slack = jnp.minimum(tallies[source_of] - 1, bound - tallies[sink]) // 2
    slack = jnp.where((source_of == ranking[0]) | (sink == ranking[0]) | (tallies[sink] == 0), 0, jnp.maximum(slack, 0))
    moved = jax.random.randint(jax.random.fold_in(own, 4), (amount // 2,), 0, 1 << 20) % (slack + 1)
    tallies = tallies.at[source_of].add(-moved).at[sink].add(moved)
    items = jnp.searchsorted(jnp.cumsum(tallies), jnp.arange(rows * top), side="right").astype(jnp.int32)
    table = items.reshape(top, rows).T
    table = table[jax.random.permutation(jax.random.fold_in(own, 1), rows)]
    turn = jax.random.randint(jax.random.fold_in(own, 2), (rows, 1), 0, top)
    return jnp.take_along_axis(table, (jnp.arange(top)[None, :] + turn) % top, axis=1)


def load_shares(amount, total, limit, slope, full):
    loads = [(1 << 20) // math.isqrt(grade ** slope) + 1 for grade in range(1, amount + 1)]
    largest = limit if full else min(limit, max(-(-total // amount), total * loads[0] // sum(loads)))
    least = 1 if total - largest >= amount - 1 else 0
    counts, rest = [largest] + [least] * (amount - 1), total - largest - least * (amount - 1)
    while rest > 0:
        free = [i for i in range(1, amount) if counts[i] < largest] or [i for i in range(1, amount) if counts[i] < limit]
        pool, left = sum([loads[i] for i in free]), rest
        for i in free:
            more = min(limit - counts[i], max(1, left * loads[i] // pool), rest)
            counts[i] = counts[i] + more
            rest = rest - more
    return np.array(counts)


def centred(stream_key, dims, width, reach, shards=(), kind=jnp.bfloat16):
    entries = width * jax.random.normal(stream_key, dims, jnp.float32)
    if shards:
        entries = entries * steps_of(stream_key, dims, shards, -0.22, 0.18)
    return jnp.clip(entries, -reach, reach).astype(kind)


def setup_inputs(seed: int = 0, part: int = 0) -> dict:
    arg_keys = jax.random.split(jax.random.key(seed), 7)
    part_keys = jax.random.split(jax.random.fold_in(arg_keys[6], part), 7)
    tokens = centred(part_keys[0], (TOKENS, D), 1.0, 6.0, ((0, 8), (1, 2)))
    expert_ids_keys = jax.random.split(jax.random.fold_in(part_keys[1], 1), TOKENS // TOK_DEV)
    expert_ids_turns = jax.random.permutation(jax.random.fold_in(part_keys[1], 3), TOKENS // TOK_DEV)
    expert_ids = jax.vmap(lambda own, number: shared_out(jax.random.fold_in(part_keys[1], 2), own, number, TOK_DEV, ROUTED, TOP, SLOT, 2))(expert_ids_keys, expert_ids_turns).reshape((TOKENS, TOP))
    route_weight = jnp.clip(0.2 + 0.8 * jax.random.uniform(part_keys[2], (TOKENS, TOP), jnp.float32) ** steps_of(part_keys[2], (TOKENS, TOP), ((0, 8),), -0.2, 0.2), 0.2, 1.0)
    gate_weight = centred(arg_keys[3], (PIECES, D, PIECE_H), D ** -0.5, 0.0625, ((0, 8), (1, 2)))
    up_weight = centred(arg_keys[4], (PIECES, D, PIECE_H), D ** -0.5, 0.0625, ((0, 8), (1, 2)))
    down_weight = centred(arg_keys[5], (PIECES, PIECE_H, D), HIDDEN_SIZE ** -0.5, 0.125, ((0, 8), (2, 2)))
    return dict(tokens=tokens, expert_ids=expert_ids, route_weight=route_weight, gate_weight=gate_weight, up_weight=up_weight, down_weight=down_weight)


def slots_of(flat_ids):
    onehot = (flat_ids[..., None] == jnp.arange(EXPERTS, dtype=jnp.int32)).astype(jnp.int32)
    before = jnp.cumsum(onehot, axis=-2) - onehot
    return jnp.sum(before * onehot, axis=-1).astype(jnp.int32)


def reference(tokens, expert_ids, route_weight, gate_weight, up_weight, down_weight):
    blocks = TOKENS // TOK_DEV
    routes = TOK_DEV * TOP
    flat_ids = expert_ids.reshape(blocks, routes)
    slot = slots_of(flat_ids)
    target = jnp.where(flat_ids < EXPERTS, flat_ids, EXPERTS).astype(jnp.int32)
    source = jnp.arange(blocks, dtype=jnp.int32)[:, None]
    position = source * SLOT + slot
    token_index = source * TOK_DEV + jnp.arange(routes, dtype=jnp.int32)[None, :] // TOP
    table = jnp.full((EXPERTS + 1, blocks * SLOT), TOKENS, jnp.int32)
    table = table.at[target.reshape(-1), position.reshape(-1)].set(token_index.reshape(-1))
    weights = jnp.zeros((EXPERTS + 1, blocks * SLOT), jnp.float32)
    weights = weights.at[target.reshape(-1), position.reshape(-1)].set(route_weight.reshape(-1))
    table = jnp.repeat(table[:EXPERTS], SPLIT, axis=0)
    weights = jnp.repeat(weights[:EXPERTS], SPLIT, axis=0)
    padded = jnp.concatenate([tokens, jnp.zeros((1, D), tokens.dtype)], axis=0)

    def one_block(total, inputs):
        rows_index, row_weight, gate_e, up_e, down_e = inputs
        chosen = padded[rows_index]
        gate = jnp.dot(chosen, gate_e, preferred_element_type=jnp.float32)
        up = jnp.dot(chosen, up_e, preferred_element_type=jnp.float32)
        hidden = (jax.nn.silu(gate) * up).astype(jnp.bfloat16)
        partial_answer = jnp.dot(hidden, down_e, preferred_element_type=jnp.float32).astype(jnp.bfloat16)
        total = total.at[rows_index].add(row_weight[:, None] * partial_answer.astype(jnp.float32))
        return total, None

    start = jnp.zeros((TOKENS + 1, D), jnp.float32)
    total, unused = lax.scan(one_block, start, (table, weights, gate_weight, up_weight, down_weight))
    return total[:TOKENS].astype(jnp.bfloat16)
```

```python
import functools

import jax
import jax.numpy as jnp
from jax import lax
from jax.experimental import pallas as pl
from jax.experimental.pallas import tpu as pltpu
from jax.sharding import PartitionSpec as P

HIDDEN_SIZE = 2048
ROUTED = 256
DIRECT = 8
BF16 = jnp.bfloat16
F32 = jnp.float32
VMEM = pl.BlockSpec(memory_space=pltpu.VMEM)


def params(*arrays):
    size = sum(a.size * a.dtype.itemsize for a in arrays)
    return pltpu.CompilerParams(vmem_limit_bytes=int(2 * size) + (6 << 20))


def shape(dims, dtype):
    return jax.ShapeDtypeStruct(dims, dtype)


def tiles(total, size):
    return [(at, min(size, total - at)) for at in range(0, total, size)]


def join(blocks):
    if len(blocks) == 1:
        return blocks[0]
    return jnp.concatenate([b.astype(F32) for b in blocks], axis=0).astype(BF16)


def spread(refs, value, at, size):
    rows = value.shape[0] // len(refs)
    for j, ref in enumerate(refs):
        ref[:, at : at + size] = value[j * rows : (j + 1) * rows].astype(BF16)


def route_kernel(slots, split, direct, ids_ref, weight_ref, tokens_ref, mix_ref, *block_refs):
    tokens, top = ids_ref.shape
    full = mix_ref.shape[1] // 3
    rows = full // split
    ids = ids_ref[...]
    weight = weight_ref[...]

    def named(count, per):
        expert = lax.broadcasted_iota(jnp.int32, (tokens, count), 1) // per
        if direct:
            expert = expert ^ lax.axis_index("expert")
        hit = jnp.zeros((tokens, count), F32)
        scale = jnp.zeros((tokens, count), F32)
        for k in range(top):
            same = ids[:, k : k + 1] == expert
            hit = jnp.where(same, 1.0, hit)
            scale = jnp.where(same, weight[:, k : k + 1], scale)
        earlier = lax.broadcasted_iota(jnp.int32, (tokens, tokens), 1) < lax.broadcasted_iota(
            jnp.int32, (tokens, tokens), 0
        )
        before = jnp.dot(
            earlier.astype(F32).astype(BF16), hit.astype(BF16), preferred_element_type=F32
        ).astype(jnp.int32)
        slot = lax.broadcasted_iota(jnp.int32, (tokens, count), 1) % slots
        return jnp.where(before == slot, hit, 0.0), scale

    chosen, scale = named(rows, slots)
    pick = chosen.astype(BF16)
    for at, size in tiles(tokens_ref.shape[1], 512):
        value = lax.dot_general(
            pick,
            tokens_ref[:, at : at + size],
            (((0,), (0,)), ((), ())),
            preferred_element_type=F32,
        )
        spread(block_refs, value, at, size)
    if split > 1:
        chosen, scale = named(full, slots * split)
    rest = chosen * scale
    for part in range(3):
        piece = rest.astype(BF16)
        mix_ref[:, part * full : (part + 1) * full] = piece
        rest = rest - piece.astype(F32)


def up_kernel(count, *refs):
    block_refs, (gate_ref, up_ref, own_ref, send_ref) = refs[:count], refs[count:]
    hidden = gate_ref.shape[1]
    rows = own_ref.shape[0]
    x = join([b[...] for b in block_refs])
    for low, high in tiles(rows, 256):
        for part, w_ref in enumerate((gate_ref, up_ref)):
            for at, size in tiles(hidden, 512):
                value = jnp.dot(
                    x[low : low + high], w_ref[:, at : at + size], preferred_element_type=F32
                )
                to = part * hidden + at
                own_ref[low : low + high, to : to + size] = value
                send_ref[low : low + high, to : to + size] = value.astype(BF16)


def down_kernel(own_ref, other_ref, down_ref, *block_refs):
    hidden = down_ref.shape[0]
    total = own_ref[...] + other_ref[...].astype(F32)
    gate, up = total[:, :hidden], total[:, hidden:]
    act = (gate / (1.0 + jnp.exp(-gate)) * up).astype(BF16)
    for at, size in tiles(down_ref.shape[1], 512):
        value = jnp.dot(act, down_ref[:, at : at + size], preferred_element_type=F32)
        spread(block_refs, value, at, size)


def mix_kernel(mix_ref, *refs):
    block_refs, out_ref = refs[:-1], refs[-1]
    full = mix_ref.shape[1] // 3
    for at, size in tiles(out_ref.shape[1], 512):
        part = join([b[:, at : at + size] for b in block_refs])
        value = jnp.zeros((out_ref.shape[0], size), F32)
        for low in (2, 1, 0):
            value += jnp.dot(
                mix_ref[:, low * full : (low + 1) * full], part, preferred_element_type=F32
            )
        out_ref[:, at : at + size] = value.astype(BF16)


def swap(blocks, devices):
    return [blocks[0]] + [
        lax.ppermute(blocks[j], "expert", [(i, i ^ j) for i in range(devices)])
        for j in range(1, devices)
    ]


def local(tokens, expert_ids, route_weight, gate_weight, up_weight, down_weight):
    devices = lax.axis_size("expert")
    split = HIDDEN_SIZE // gate_weight.shape[2]
    experts = devices // split
    count, width = tokens.shape
    top = expert_ids.shape[1]
    slots = min(max(4, 2 * count * top // ROUTED), count)
    hidden = gate_weight.shape[2]
    rows = devices * slots
    direct = split == 1 and devices <= DIRECT and devices & (devices - 1) == 0
    near = functools.partial(pltpu.with_memory_space_constraint, memory_space=pltpu.VMEM)

    parts = devices if direct else 1
    sent = experts * slots // parts
    mix, *send = pl.pallas_call(
        functools.partial(route_kernel, slots, split, direct),
        in_specs=[VMEM] * 3,
        out_specs=[VMEM] * (1 + parts),
        out_shape=[shape((count, 3 * rows), BF16)] + [shape((sent, width), BF16)] * parts,
        compiler_params=params(tokens, shape((count, 8 * rows), F32)),
        name="route",
    )(expert_ids, route_weight, tokens)
    if direct:
        arrived = swap(send, devices)
    else:
        spread_out = jnp.repeat(send[0].reshape(experts, slots, width), split, axis=0)
        arrived = [
            lax.all_to_all(spread_out, "expert", 0, 0, tiled=True).reshape(rows, width)
        ]

    own, give = pl.pallas_call(
        functools.partial(up_kernel, parts),
        in_specs=[VMEM] * (parts + 2),
        out_specs=[VMEM] * 2,
        out_shape=[shape((rows, 2 * hidden), F32), shape((rows, 2 * hidden), BF16)],
        compiler_params=params(shape((rows, width), F32), shape((rows, 2 * hidden), F32)),
        name="up",
    )(*arrived, near(gate_weight[0]), near(up_weight[0]))
    cores = lax.axis_size("tensor")
    other = lax.ppermute(give, "tensor", [(i, (i + 1) % cores) for i in range(cores)])
    answer = pl.pallas_call(
        down_kernel,
        in_specs=[VMEM] * 3,
        out_specs=[VMEM] * parts,
        out_shape=[shape((rows // parts, width), BF16)] * parts,
        compiler_params=params(shape((rows, 4 * hidden), F32), shape((rows, width), F32)),
        name="down",
    )(own, other, near(down_weight[0]))
    if direct:
        back = swap(answer, devices)
    else:
        back = [
            lax.all_to_all(
                answer[0].reshape(devices, slots, width), "expert", 0, 0, tiled=True
            ).reshape(rows, width)
        ]
    return pl.pallas_call(
        mix_kernel,
        in_specs=[VMEM] * (1 + parts),
        out_specs=VMEM,
        out_shape=shape((count, width), BF16),
        compiler_params=params(mix, tokens, shape((rows, width), BF16)),
        name="mix",
    )(mix, *back)


def solution(mesh):
    return jax.shard_map(
        local,
        mesh=mesh,
        in_specs=(
            P(("groups", "expert"), "tensor"),
            P(("groups", "expert"), None),
            P(("groups", "expert"), None),
            P("expert", "tensor", None),
            P("expert", "tensor", None),
            P("expert", None, "tensor"),
        ),
        out_specs=P(("groups", "expert"), "tensor"),
        check_vma=False,
    )
```

```python
import functools

import jax
import jax.numpy as jnp
from jax import lax
from jax.experimental import pallas as pl
from jax.experimental.pallas import tpu as pltpu
from jax.sharding import PartitionSpec as P

HIDDEN_SIZE = 2048
ROUTED = 256
ORDER = (0, 4, 5, 6, 7, 2, 3, 1)
BF16 = jnp.bfloat16
F32 = jnp.float32
VMEM = pl.BlockSpec(memory_space=pltpu.VMEM)


def params(*arrays):
    size = sum(a.size * a.dtype.itemsize for a in arrays)
    return pltpu.CompilerParams(vmem_limit_bytes=int(2 * size) + (6 << 20))


def shape(dims, dtype):
    return jax.ShapeDtypeStruct(dims, dtype)


def tiles(total, size):
    return [(at, min(size, total - at)) for at in range(0, total, size)]


def join(blocks):
    if len(blocks) == 1:
        return blocks[0]
    return jnp.concatenate([b.astype(F32) for b in blocks], axis=0).astype(BF16)


def padded(x):
    short = 128 - x.shape[0]
    return x if short <= 0 else jnp.concatenate([x, jnp.zeros((short, x.shape[1]), x.dtype)], axis=0)


def partner(place):
    return sum(jnp.where(place == at, j, 0) for at, j in enumerate(ORDER) if j)


def spread(refs, value, at, size):
    rows = value.shape[0] // len(refs)
    for j, ref in enumerate(refs):
        ref[:, at : at + size] = value[j * rows : (j + 1) * rows].astype(BF16)


def route_kernel(slots, split, direct, ids_hbm, weight_hbm, tokens_hbm, share_ref, *rest_refs):
    *block_refs, ids_ref, weight_ref, tokens_ref, sems = rest_refs
    top, tokens = ids_ref.shape
    columns = tiles(tokens_ref.shape[1], 512)
    copies = [
        pltpu.make_async_copy(ids_hbm, ids_ref, sems.at[0]),
        pltpu.make_async_copy(weight_hbm, weight_ref, sems.at[1]),
    ] + [
        pltpu.make_async_copy(
            tokens_hbm.at[:, at : at + size], tokens_ref.at[:, at : at + size], sems.at[2 + i]
        )
        for i, (at, size) in enumerate(columns)
    ]
    for copy in copies:
        copy.start()
    copies[0].wait()
    copies[1].wait()
    full = share_ref.shape[0]
    rows = full // split

    def named(count, per):
        expert = lax.broadcasted_iota(jnp.int32, (count, tokens), 0) // per
        if direct:
            expert = partner(expert) ^ lax.axis_index("expert")
        hit = jnp.zeros((count, tokens), F32)
        scale = jnp.zeros((count, tokens), F32)
        for k in range(top):
            same = ids_ref[k : k + 1, :] == expert
            hit = jnp.where(same, 1.0, hit)
            scale = jnp.where(same, weight_ref[k : k + 1, :], scale)
        earlier = lax.broadcasted_iota(jnp.int32, (tokens, tokens), 0) < lax.broadcasted_iota(
            jnp.int32, (tokens, tokens), 1
        )
        before = jnp.dot(
            hit.astype(BF16), earlier.astype(F32).astype(BF16), preferred_element_type=F32
        ).astype(jnp.int32)
        slot = lax.broadcasted_iota(jnp.int32, (count, tokens), 0) % slots
        return jnp.where(before == slot, hit, 0.0), scale

    chosen, scale = named(rows, slots)
    pick = chosen.astype(BF16)
    for i, (at, size) in enumerate(columns):
        copies[2 + i].wait()
        value = jnp.dot(pick, tokens_ref[:, at : at + size], preferred_element_type=F32)
        spread(block_refs, value, at, size)
    if split > 1:
        chosen, scale = named(full, slots * split)
    share_ref[...] = chosen * scale


def split_weights(share_ref, mix_ref):
    full = share_ref.shape[0]
    rest = share_ref[...].T
    for part in range(3):
        piece = rest.astype(BF16)
        mix_ref[:, part * full : (part + 1) * full] = piece
        rest = rest - piece.astype(F32)


def up_kernel(count, *refs):
    block_refs = refs[:count]
    share_ref, gate_ref, up_ref, own_ref, send_ref, mix_ref = refs[count:]
    split_weights(share_ref, mix_ref)
    hidden = gate_ref.shape[1]
    rows = own_ref.shape[0]
    x = padded(join([b[...] for b in block_refs]))
    for low, high in tiles(x.shape[0], 256):
        for part, w_ref in enumerate((gate_ref, up_ref)):
            for at, size in tiles(hidden, 512):
                value = jnp.dot(
                    x[low : low + high], w_ref[:, at : at + size], preferred_element_type=F32
                )[: min(high, rows)]
                to = part * hidden + at
                own_ref[low : low + value.shape[0], to : to + size] = value
                send_ref[low : low + value.shape[0], to : to + size] = value.astype(BF16)


def down_kernel(own_ref, other_ref, down_ref, *block_refs):
    rows, hidden = own_ref.shape[0], down_ref.shape[0]
    total = own_ref[...] + other_ref[...].astype(F32)
    gate, up = total[:, :hidden], total[:, hidden:]
    act = padded((gate / (1.0 + jnp.exp(-gate)) * up).astype(BF16))
    for at, size in tiles(down_ref.shape[1], 512):
        value = jnp.dot(act, down_ref[:, at : at + size], preferred_element_type=F32)[:rows]
        spread(block_refs, value, at, size)


def mix_kernel(count, mix_ref, *refs):
    block_refs, (out_hbm, out_ref, sems) = refs[:count], refs[count:]
    mix = mix_ref[...]
    copies = []
    for i, (at, size) in enumerate(tiles(out_ref.shape[1], 512)):
        part = join([b[:, at : at + size] for b in block_refs])
        value = jnp.dot(
            mix, jnp.concatenate([part] * 3, axis=0), preferred_element_type=F32
        )
        out_ref[:, at : at + size] = value.astype(BF16)
        copy = pltpu.make_async_copy(
            out_ref.at[:, at : at + size], out_hbm.at[:, at : at + size], sems.at[i]
        )
        copy.start()
        copies.append(copy)
    for copy in copies:
        copy.wait()


def swap(blocks, devices):
    return [
        lax.ppermute(block, "expert", [(i, i ^ j) for i in range(devices)]) if j else block
        for block, j in zip(blocks, ORDER)
    ]


def local(tokens, expert_ids, route_weight, gate_weight, up_weight, down_weight):
    devices = lax.axis_size("expert")
    split = HIDDEN_SIZE // gate_weight.shape[2]
    experts = devices // split
    count, width = tokens.shape
    top = expert_ids.shape[1]
    slots = min(max(4, 2 * count * top // ROUTED), count)
    hidden = gate_weight.shape[2]
    rows = devices * slots
    direct = split == 1 and devices == len(ORDER)
    near = functools.partial(pltpu.with_memory_space_constraint, memory_space=pltpu.VMEM)
    far = functools.partial(pltpu.with_memory_space_constraint, memory_space=pltpu.HBM)

    parts = devices if direct else 1
    sent = experts * slots // parts
    share, *send = pl.pallas_call(
        functools.partial(route_kernel, slots, split, direct),
        in_specs=[pl.BlockSpec(memory_space=pltpu.HBM)] * 3,
        out_specs=[VMEM] * (1 + parts),
        out_shape=[shape((rows, count), F32)] + [shape((sent, width), BF16)] * parts,
        scratch_shapes=[
            pltpu.VMEM((top, count), jnp.int32),
            pltpu.VMEM((top, count), F32),
            pltpu.VMEM((count, width), BF16),
            pltpu.SemaphoreType.DMA((2 + pl.cdiv(width, 512),)),
        ],
        compiler_params=params(tokens, shape((count, 8 * rows), F32)),
        cost_estimate=pl.CostEstimate(flops=int(3e10), bytes_accessed=0, transcendentals=0),
        name="route",
    )(far(expert_ids.T), far(route_weight.T), far(tokens))
    if direct:
        arrived = swap(send, devices)
    else:
        spread_out = jnp.repeat(send[0].reshape(experts, slots, width), split, axis=0)
        arrived = [
            lax.all_to_all(spread_out, "expert", 0, 0, tiled=True).reshape(rows, width)
        ]

    own, give, mix = pl.pallas_call(
        functools.partial(up_kernel, parts),
        in_specs=[VMEM] * (parts + 3),
        out_specs=[VMEM] * 3,
        out_shape=[
            shape((rows, 2 * hidden), F32),
            shape((rows, 2 * hidden), BF16),
            shape((count, 3 * rows), BF16),
        ],
        compiler_params=params(shape((rows, width), F32), shape((rows, 2 * hidden), F32)),
        name="up",
    )(*arrived, share, near(gate_weight[0]), near(up_weight[0]))
    cores = lax.axis_size("tensor")
    other = lax.ppermute(give, "tensor", [(i, (i + 1) % cores) for i in range(cores)])
    answer = pl.pallas_call(
        down_kernel,
        in_specs=[VMEM] * 3,
        out_specs=[VMEM] * parts,
        out_shape=[shape((rows // parts, width), BF16)] * parts,
        compiler_params=params(shape((rows, 4 * hidden), F32), shape((rows, width), F32)),
        name="down",
    )(own, other, near(down_weight[0]))
    if direct:
        back = swap(answer, devices)
    else:
        back = [
            lax.all_to_all(
                answer[0].reshape(devices, slots, width), "expert", 0, 0, tiled=True
            ).reshape(rows, width)
        ]
    return pl.pallas_call(
        functools.partial(mix_kernel, parts),
        in_specs=[VMEM] * (1 + parts),
        out_specs=pl.BlockSpec(memory_space=pltpu.HBM),
        scratch_shapes=[
            pltpu.VMEM((count, width), BF16),
            pltpu.SemaphoreType.DMA((pl.cdiv(width, 512),)),
        ],
        out_shape=shape((count, width), BF16),
        compiler_params=params(mix, tokens, shape((rows, width), BF16)),
        name="mix",
    )(mix, *back)


def solution(mesh):
    return jax.shard_map(
        local,
        mesh=mesh,
        in_specs=(
            P(("groups", "expert"), "tensor"),
            P(("groups", "expert"), None),
            P(("groups", "expert"), None),
            P("expert", "tensor", None),
            P("expert", "tensor", None),
            P("expert", None, "tensor"),
        ),
        out_specs=P(("groups", "expert"), "tensor"),
        check_vma=False,
    )
```

```python
import functools

import jax
import jax.numpy as jnp
from jax import lax
from jax.experimental import pallas as pl
from jax.experimental.pallas import tpu as pltpu
from jax.sharding import PartitionSpec as P

HIDDEN_SIZE = 2048
ROUTED = 256
ORDER = (0, 7, 6, 5, 3, 4, 2, 1)
BF16 = jnp.bfloat16
F32 = jnp.float32
VMEM = pl.BlockSpec(memory_space=pltpu.VMEM)


def params(*arrays):
    size = sum(a.size * a.dtype.itemsize for a in arrays)
    return pltpu.CompilerParams(vmem_limit_bytes=int(2 * size) + (6 << 20))


def shape(dims, dtype):
    return jax.ShapeDtypeStruct(dims, dtype)


def tiles(total, size):
    return [(at, min(size, total - at)) for at in range(0, total, size)]


def join(blocks):
    if len(blocks) == 1:
        return blocks[0]
    return jnp.concatenate([b.astype(F32) for b in blocks], axis=0).astype(BF16)


def padded(x):
    short = 128 - x.shape[0]
    return x if short <= 0 else jnp.concatenate([x, jnp.zeros((short, x.shape[1]), x.dtype)], axis=0)


def partner(place):
    return sum(jnp.where(place == at, j, 0) for at, j in enumerate(ORDER) if j)


def spread(refs, value, at, size):
    rows = value.shape[0] // len(refs)
    for j, ref in enumerate(refs):
        ref[:, at : at + size] = value[j * rows : (j + 1) * rows].astype(BF16)


def route_kernel(slots, split, direct, ids_hbm, weight_hbm, tokens_hbm, share_ref, *rest_refs):
    *block_refs, ids_ref, weight_ref, tokens_ref, sems = rest_refs
    top, tokens = ids_ref.shape
    columns = tiles(tokens_ref.shape[1], 512)
    copies = [
        pltpu.make_async_copy(ids_hbm, ids_ref, sems.at[0]),
        pltpu.make_async_copy(weight_hbm, weight_ref, sems.at[1]),
    ] + [
        pltpu.make_async_copy(
            tokens_hbm.at[:, at : at + size], tokens_ref.at[:, at : at + size], sems.at[2 + i]
        )
        for i, (at, size) in enumerate(columns)
    ]
    for copy in copies:
        copy.start()
    copies[0].wait()
    copies[1].wait()
    full = share_ref.shape[0]
    rows = full // split

    def named(count, per):
        expert = lax.broadcasted_iota(jnp.int32, (count, tokens), 0) // per
        if direct:
            expert = partner(expert) ^ lax.axis_index("expert")
        hit = jnp.zeros((count, tokens), F32)
        scale = jnp.zeros((count, tokens), F32)
        for k in range(top):
            same = ids_ref[k : k + 1, :] == expert
            hit = jnp.where(same, 1.0, hit)
            scale = jnp.where(same, weight_ref[k : k + 1, :], scale)
        earlier = lax.broadcasted_iota(jnp.int32, (tokens, tokens), 0) < lax.broadcasted_iota(
            jnp.int32, (tokens, tokens), 1
        )
        before = jnp.dot(
            hit.astype(BF16), earlier.astype(F32).astype(BF16), preferred_element_type=F32
        ).astype(jnp.int32)
        slot = lax.broadcasted_iota(jnp.int32, (count, tokens), 0) % slots
        return jnp.where(before == slot, hit, 0.0), scale

    chosen, scale = named(rows, slots)
    pick = chosen.astype(BF16)
    for i, (at, size) in enumerate(columns):
        copies[2 + i].wait()
        value = jnp.dot(pick, tokens_ref[:, at : at + size], preferred_element_type=F32)
        spread(block_refs, value, at, size)
    if split > 1:
        chosen, scale = named(full, slots * split)
    share_ref[...] = chosen * scale


def split_weights(share_ref, mix_ref):
    full = share_ref.shape[0]
    rest = share_ref[...].T
    for part in range(3):
        piece = rest.astype(BF16)
        mix_ref[:, part * full : (part + 1) * full] = piece
        rest = rest - piece.astype(F32)


def up_kernel(count, *refs):
    block_refs = refs[:count]
    share_ref, gate_ref, up_ref, own_ref, send_ref, mix_ref = refs[count:]
    split_weights(share_ref, mix_ref)
    hidden = gate_ref.shape[1]
    rows = own_ref.shape[0]
    x = padded(join([b[...] for b in block_refs]))
    for low, high in tiles(x.shape[0], 256):
        for part, w_ref in enumerate((gate_ref, up_ref)):
            for at, size in tiles(hidden, 512):
                value = jnp.dot(
                    x[low : low + high], w_ref[:, at : at + size], preferred_element_type=F32
                )[: min(high, rows)]
                to = part * hidden + at
                own_ref[low : low + value.shape[0], to : to + size] = value
                send_ref[low : low + value.shape[0], to : to + size] = value.astype(BF16)


def down_kernel(own_ref, other_ref, down_ref, *block_refs):
    rows, hidden = own_ref.shape[0], down_ref.shape[0]
    total = own_ref[...] + other_ref[...].astype(F32)
    gate, up = total[:, :hidden], total[:, hidden:]
    act = padded((gate / (1.0 + jnp.exp(-gate)) * up).astype(BF16))
    for at, size in tiles(down_ref.shape[1], 512):
        value = jnp.dot(act, down_ref[:, at : at + size], preferred_element_type=F32)[:rows]
        spread(block_refs, value, at, size)


def mix_kernel(count, mix_ref, *refs):
    block_refs, (out_hbm, out_ref, sems) = refs[:count], refs[count:]
    mix = mix_ref[...]
    copies = []
    for i, (at, size) in enumerate(tiles(out_ref.shape[1], 512)):
        part = join([b[:, at : at + size] for b in block_refs])
        value = jnp.dot(
            mix, jnp.concatenate([part] * 3, axis=0), preferred_element_type=F32
        )
        out_ref[:, at : at + size] = value.astype(BF16)
        copy = pltpu.make_async_copy(
            out_ref.at[:, at : at + size], out_hbm.at[:, at : at + size], sems.at[i]
        )
        copy.start()
        copies.append(copy)
    for copy in copies:
        copy.wait()


def swap(blocks, devices):
    return [
        lax.ppermute(block, "expert", [(i, i ^ j) for i in range(devices)]) if j else block
        for block, j in zip(blocks, ORDER)
    ]


def local(tokens, expert_ids, route_weight, gate_weight, up_weight, down_weight):
    devices = lax.axis_size("expert")
    split = HIDDEN_SIZE // gate_weight.shape[2]
    experts = devices // split
    count, width = tokens.shape
    top = expert_ids.shape[1]
    slots = min(max(4, 2 * count * top // ROUTED), count)
    hidden = gate_weight.shape[2]
    rows = devices * slots
    direct = split == 1 and devices == len(ORDER)
    near = functools.partial(pltpu.with_memory_space_constraint, memory_space=pltpu.VMEM)
    far = functools.partial(pltpu.with_memory_space_constraint, memory_space=pltpu.HBM)

    parts = devices if direct else 1
    sent = experts * slots // parts
    share, *send = pl.pallas_call(
        functools.partial(route_kernel, slots, split, direct),
        in_specs=[pl.BlockSpec(memory_space=pltpu.HBM)] * 3,
        out_specs=[VMEM] * (1 + parts),
        out_shape=[shape((rows, count), F32)] + [shape((sent, width), BF16)] * parts,
        scratch_shapes=[
            pltpu.VMEM((top, count), jnp.int32),
            pltpu.VMEM((top, count), F32),
            pltpu.VMEM((count, width), BF16),
            pltpu.SemaphoreType.DMA((2 + pl.cdiv(width, 512),)),
        ],
        compiler_params=params(tokens, shape((count, 8 * rows), F32)),
        cost_estimate=pl.CostEstimate(flops=int(3e10), bytes_accessed=0, transcendentals=0),
        name="route",
    )(far(expert_ids.T), far(route_weight.T), far(tokens))
    if direct:
        arrived = swap(send, devices)
    else:
        spread_out = jnp.repeat(send[0].reshape(experts, slots, width), split, axis=0)
        arrived = [
            lax.all_to_all(spread_out, "expert", 0, 0, tiled=True).reshape(rows, width)
        ]

    own, give, mix = pl.pallas_call(
        functools.partial(up_kernel, parts),
        in_specs=[VMEM] * (parts + 3),
        out_specs=[VMEM] * 3,
        out_shape=[
            shape((rows, 2 * hidden), F32),
            shape((rows, 2 * hidden), BF16),
            shape((count, 3 * rows), BF16),
        ],
        compiler_params=params(shape((rows, width), F32), shape((rows, 2 * hidden), F32)),
        name="up",
    )(*arrived, share, near(gate_weight[0]), near(up_weight[0]))
    cores = lax.axis_size("tensor")
    other = lax.ppermute(give, "tensor", [(i, (i + 1) % cores) for i in range(cores)])
    answer = pl.pallas_call(
        down_kernel,
        in_specs=[VMEM] * 3,
        out_specs=[VMEM] * parts,
        out_shape=[shape((rows // parts, width), BF16)] * parts,
        compiler_params=params(shape((rows, 4 * hidden), F32), shape((rows, width), F32)),
        name="down",
    )(own, other, near(down_weight[0]))
    if direct:
        back = swap(answer, devices)
    else:
        back = [
            lax.all_to_all(
                answer[0].reshape(devices, slots, width), "expert", 0, 0, tiled=True
            ).reshape(rows, width)
        ]
    return pl.pallas_call(
        functools.partial(mix_kernel, parts),
        in_specs=[VMEM] * (1 + parts),
        out_specs=pl.BlockSpec(memory_space=pltpu.HBM),
        scratch_shapes=[
            pltpu.VMEM((count, width), BF16),
            pltpu.SemaphoreType.DMA((pl.cdiv(width, 512),)),
        ],
        out_shape=shape((count, width), BF16),
        compiler_params=params(mix, tokens, shape((rows, width), BF16)),
        name="mix",
    )(mix, *back)


def solution(mesh):
    return jax.shard_map(
        local,
        mesh=mesh,
        in_specs=(
            P(("groups", "expert"), "tensor"),
            P(("groups", "expert"), None),
            P(("groups", "expert"), None),
            P("expert", "tensor", None),
            P("expert", "tensor", None),
            P("expert", None, "tensor"),
        ),
        out_specs=P(("groups", "expert"), "tensor"),
        check_vma=False,
    )
```

```python
import functools

import jax
import jax.numpy as jnp
from jax import lax
from jax.experimental import pallas as pl
from jax.experimental.pallas import tpu as pltpu
from jax.sharding import PartitionSpec as P

HIDDEN_SIZE = 2048
ROUTED = 256
ORDER = (0, 7, 6, 5, 3, 4, 2, 1)
BF16 = jnp.bfloat16
F32 = jnp.float32
VMEM = pl.BlockSpec(memory_space=pltpu.VMEM)


def params(*arrays):
    size = sum(a.size * a.dtype.itemsize for a in arrays)
    return pltpu.CompilerParams(vmem_limit_bytes=int(1.25 * size) + (3 << 20))


def shape(dims, dtype):
    return jax.ShapeDtypeStruct(dims, dtype)


def tiles(total, size):
    return [(at, min(size, total - at)) for at in range(0, total, size)]


def join(blocks):
    if len(blocks) == 1:
        return blocks[0]
    return jnp.concatenate([b.astype(F32) for b in blocks], axis=0).astype(BF16)


def padded(x):
    short = 128 - x.shape[0]
    return x if short <= 0 else jnp.concatenate([x, jnp.zeros((short, x.shape[1]), x.dtype)], axis=0)


def partner(place):
    return sum(jnp.where(place == at, j, 0) for at, j in enumerate(ORDER) if j)


def spread(refs, value, at, size):
    rows = value.shape[0] // len(refs)
    for j, ref in enumerate(refs):
        ref[:, at : at + size] = value[j * rows : (j + 1) * rows].astype(BF16)


def route_kernel(
    slots, split, direct, ids_hbm, weight_hbm, tokens_hbm, pick_ref, share_ref, tokens_ref, *rest
):
    ids_ref, weight_ref, sems = rest
    top, tokens = ids_ref.shape
    full = share_ref.shape[0]
    rows = full // split
    copies = [
        pltpu.make_async_copy(ids_hbm, ids_ref, sems.at[0]),
        pltpu.make_async_copy(weight_hbm, weight_ref, sems.at[1]),
        pltpu.make_async_copy(tokens_hbm, tokens_ref, sems.at[2]),
    ]
    for copy in copies:
        copy.start()
    copies[0].wait()
    copies[1].wait()

    def named(count, per):
        expert = lax.broadcasted_iota(jnp.int32, (count, tokens), 0) // per
        if direct:
            expert = partner(expert) ^ lax.axis_index("expert")
        hit = jnp.zeros((count, tokens), F32)
        scale = jnp.zeros((count, tokens), F32)
        for k in range(top):
            same = ids_ref[k : k + 1, :] == expert
            hit = jnp.where(same, 1.0, hit)
            scale = jnp.where(same, weight_ref[k : k + 1, :], scale)
        earlier = lax.broadcasted_iota(jnp.int32, (tokens, tokens), 0) < lax.broadcasted_iota(
            jnp.int32, (tokens, tokens), 1
        )
        before = jnp.dot(
            hit.astype(BF16), earlier.astype(F32).astype(BF16), preferred_element_type=F32
        ).astype(jnp.int32)
        slot = lax.broadcasted_iota(jnp.int32, (count, tokens), 0) % slots
        return jnp.where(before == slot, hit, 0.0), scale

    chosen, scale = named(rows, slots)
    pick_ref[...] = chosen.astype(BF16)
    if split > 1:
        chosen, scale = named(full, slots * split)
    share_ref[...] = chosen * scale
    copies[2].wait()


def send_kernel(pick_ref, tokens_ref, *block_refs):
    pick = pick_ref[...]
    for at, size in tiles(tokens_ref.shape[1], 512):
        value = jnp.dot(pick, tokens_ref[:, at : at + size], preferred_element_type=F32)
        spread(block_refs, value, at, size)


def split_weights(share_ref, mix_ref):
    full = share_ref.shape[0]
    rest = share_ref[...].T
    for part in range(3):
        piece = rest.astype(BF16)
        mix_ref[:, part * full : (part + 1) * full] = piece
        rest = rest - piece.astype(F32)


def up_kernel(count, *refs):
    block_refs = refs[:count]
    share_ref, gate_ref, up_ref, own_ref, send_ref, mix_ref = refs[count:]
    split_weights(share_ref, mix_ref)
    hidden = gate_ref.shape[1]
    rows = own_ref.shape[0]
    x = padded(join([b[...] for b in block_refs]))
    for low, high in tiles(x.shape[0], 256):
        for part, w_ref in enumerate((gate_ref, up_ref)):
            for at, size in tiles(hidden, 512):
                value = jnp.dot(
                    x[low : low + high], w_ref[:, at : at + size], preferred_element_type=F32
                )[: min(high, rows)]
                to = part * hidden + at
                own_ref[low : low + value.shape[0], to : to + size] = value
                send_ref[low : low + value.shape[0], to : to + size] = value.astype(BF16)


def down_kernel(own_ref, other_ref, down_ref, *block_refs):
    rows, hidden = own_ref.shape[0], down_ref.shape[0]
    total = own_ref[...] + other_ref[...].astype(F32)
    gate, up = total[:, :hidden], total[:, hidden:]
    act = padded((gate / (1.0 + jnp.exp(-gate)) * up).astype(BF16))
    for at, size in tiles(down_ref.shape[1], 512):
        value = jnp.dot(act, down_ref[:, at : at + size], preferred_element_type=F32)[:rows]
        spread(block_refs, value, at, size)


def mix_kernel(count, mix_ref, *refs):
    block_refs, (out_hbm, out_ref, sems) = refs[:count], refs[count:]
    mix = mix_ref[...]
    copies = []
    for i, (at, size) in enumerate(tiles(out_ref.shape[1], 512)):
        part = join([b[:, at : at + size] for b in block_refs])
        value = jnp.dot(
            mix, jnp.concatenate([part] * 3, axis=0), preferred_element_type=F32
        )
        out_ref[:, at : at + size] = value.astype(BF16)
        copy = pltpu.make_async_copy(
            out_ref.at[:, at : at + size], out_hbm.at[:, at : at + size], sems.at[i]
        )
        copy.start()
        copies.append(copy)
    for copy in copies:
        copy.wait()


def swap(blocks, devices):
    return [
        lax.ppermute(block, "expert", [(i, i ^ j) for i in range(devices)]) if j else block
        for block, j in zip(blocks, ORDER)
    ]


def local(tokens, expert_ids, route_weight, gate_weight, up_weight, down_weight):
    devices = lax.axis_size("expert")
    split = HIDDEN_SIZE // gate_weight.shape[2]
    experts = devices // split
    count, width = tokens.shape
    top = expert_ids.shape[1]
    slots = min(max(4, 2 * count * top // ROUTED), count)
    hidden = gate_weight.shape[2]
    rows = devices * slots
    direct = split == 1 and devices == len(ORDER)
    near = functools.partial(pltpu.with_memory_space_constraint, memory_space=pltpu.VMEM)
    far = functools.partial(pltpu.with_memory_space_constraint, memory_space=pltpu.HBM)

    parts = devices if direct else 1
    sent = experts * slots // parts
    pick, share, held = pl.pallas_call(
        functools.partial(route_kernel, slots, split, direct),
        in_specs=[pl.BlockSpec(memory_space=pltpu.HBM)] * 3,
        out_specs=[VMEM] * 3,
        out_shape=[
            shape((experts * slots, count), BF16),
            shape((rows, count), F32),
            shape((count, width), BF16),
        ],
        scratch_shapes=[
            pltpu.VMEM((top, count), jnp.int32),
            pltpu.VMEM((top, count), F32),
            pltpu.SemaphoreType.DMA((3,)),
        ],
        compiler_params=params(tokens, shape((count, 8 * rows), F32)),
        cost_estimate=pl.CostEstimate(flops=int(1e6), bytes_accessed=0, transcendentals=0),
        name="route",
    )(far(expert_ids.T), far(route_weight.T), far(tokens))
    send = pl.pallas_call(
        send_kernel,
        in_specs=[VMEM] * 2,
        out_specs=[VMEM] * parts,
        out_shape=[shape((sent, width), BF16)] * parts,
        compiler_params=params(tokens, tokens),
        cost_estimate=pl.CostEstimate(flops=int(3e10), bytes_accessed=0, transcendentals=0),
        name="send",
    )(pick, held)
    if direct:
        arrived = swap(send, devices)
    else:
        spread_out = jnp.repeat(send[0].reshape(experts, slots, width), split, axis=0)
        arrived = [
            lax.all_to_all(spread_out, "expert", 0, 0, tiled=True).reshape(rows, width)
        ]

    own, give, mix = pl.pallas_call(
        functools.partial(up_kernel, parts),
        in_specs=[VMEM] * (parts + 3),
        out_specs=[VMEM] * 3,
        out_shape=[
            shape((rows, 2 * hidden), F32),
            shape((rows, 2 * hidden), BF16),
            shape((count, 3 * rows), BF16),
        ],
        compiler_params=params(shape((rows, width), F32), shape((rows, 2 * hidden), F32)),
        name="up",
    )(*arrived, share, near(gate_weight[0]), near(up_weight[0]))
    cores = lax.axis_size("tensor")
    other = lax.ppermute(give, "tensor", [(i, (i + 1) % cores) for i in range(cores)])
    answer = pl.pallas_call(
        down_kernel,
        in_specs=[VMEM] * 3,
        out_specs=[VMEM] * parts,
        out_shape=[shape((rows // parts, width), BF16)] * parts,
        compiler_params=params(shape((rows, 4 * hidden), F32), shape((rows, width), F32)),
        name="down",
    )(own, other, near(down_weight[0]))
    if direct:
        back = swap(answer, devices)
    else:
        back = [
            lax.all_to_all(
                answer[0].reshape(devices, slots, width), "expert", 0, 0, tiled=True
            ).reshape(rows, width)
        ]
    return pl.pallas_call(
        functools.partial(mix_kernel, parts),
        in_specs=[VMEM] * (1 + parts),
        out_specs=pl.BlockSpec(memory_space=pltpu.HBM),
        scratch_shapes=[
            pltpu.VMEM((count, width), BF16),
            pltpu.SemaphoreType.DMA((pl.cdiv(width, 512),)),
        ],
        out_shape=shape((count, width), BF16),
        compiler_params=params(mix, tokens, shape((rows, width), BF16)),
        name="mix",
    )(mix, *back)


def solution(mesh):
    return jax.shard_map(
        local,
        mesh=mesh,
        in_specs=(
            P(("groups", "expert"), "tensor"),
            P(("groups", "expert"), None),
            P(("groups", "expert"), None),
            P("expert", "tensor", None),
            P("expert", "tensor", None),
            P("expert", None, "tensor"),
        ),
        out_specs=P(("groups", "expert"), "tensor"),
        check_vma=False,
    )
```

```python
import functools

import jax
import jax.numpy as jnp
from jax import lax
from jax.experimental import pallas as pl
from jax.experimental.pallas import tpu as pltpu
from jax.sharding import PartitionSpec as P

HIDDEN_SIZE = 2048
ROUTED = 256
ORDER = (0, 7, 6, 5, 3, 4, 2, 1)
RETURN = (0, 5, 6, 3, 7, 4, 2, 1)
BF16 = jnp.bfloat16
F32 = jnp.float32
VMEM = pl.BlockSpec(memory_space=pltpu.VMEM)


def params(*arrays):
    size = sum(a.size * a.dtype.itemsize for a in arrays)
    return pltpu.CompilerParams(vmem_limit_bytes=int(1.25 * size) + (3 << 20))


def shape(dims, dtype):
    return jax.ShapeDtypeStruct(dims, dtype)


def tiles(total, size):
    return [(at, min(size, total - at)) for at in range(0, total, size)]


def join(blocks):
    if len(blocks) == 1:
        return blocks[0]
    return jnp.concatenate([b.astype(F32) for b in blocks], axis=0).astype(BF16)


def padded(x):
    short = 128 - x.shape[0]
    return x if short <= 0 else jnp.concatenate([x, jnp.zeros((short, x.shape[1]), x.dtype)], axis=0)


def partner(place):
    return sum(jnp.where(place == at, j, 0) for at, j in enumerate(ORDER) if j)


def spread(refs, value, at, size):
    rows = value.shape[0] // len(refs)
    for j, ref in enumerate(refs):
        ref[:, at : at + size] = value[j * rows : (j + 1) * rows].astype(BF16)


def route_kernel(
    slots, split, direct, ids_hbm, weight_hbm, tokens_hbm, pick_ref, share_ref, tokens_ref, *rest
):
    ids_ref, weight_ref, sems = rest
    top, tokens = ids_ref.shape
    full = share_ref.shape[0]
    rows = full // split
    copies = [
        pltpu.make_async_copy(ids_hbm, ids_ref, sems.at[0]),
        pltpu.make_async_copy(weight_hbm, weight_ref, sems.at[1]),
        pltpu.make_async_copy(tokens_hbm, tokens_ref, sems.at[2]),
    ]
    for copy in copies:
        copy.start()
    copies[0].wait()
    copies[1].wait()

    def named(count, per):
        expert = lax.broadcasted_iota(jnp.int32, (count, tokens), 0) // per
        if direct:
            expert = partner(expert) ^ lax.axis_index("expert")
        hit = jnp.zeros((count, tokens), F32)
        scale = jnp.zeros((count, tokens), F32)
        for k in range(top):
            same = ids_ref[k : k + 1, :] == expert
            hit = jnp.where(same, 1.0, hit)
            scale = jnp.where(same, weight_ref[k : k + 1, :], scale)
        earlier = lax.broadcasted_iota(jnp.int32, (tokens, tokens), 0) < lax.broadcasted_iota(
            jnp.int32, (tokens, tokens), 1
        )
        before = jnp.dot(
            hit.astype(BF16), earlier.astype(F32).astype(BF16), preferred_element_type=F32
        ).astype(jnp.int32)
        slot = lax.broadcasted_iota(jnp.int32, (count, tokens), 0) % slots
        return jnp.where(before == slot, hit, 0.0), scale

    chosen, scale = named(rows, slots)
    pick_ref[...] = chosen.astype(BF16)
    if split > 1:
        chosen, scale = named(full, slots * split)
    share_ref[...] = chosen * scale
    copies[2].wait()


def send_kernel(pick_ref, tokens_ref, *block_refs):
    pick = pick_ref[...]
    for at, size in tiles(tokens_ref.shape[1], 512):
        value = jnp.dot(pick, tokens_ref[:, at : at + size], preferred_element_type=F32)
        spread(block_refs, value, at, size)


def split_weights(share_ref, mix_ref):
    full = share_ref.shape[0]
    rest = share_ref[...].T
    for part in range(3):
        piece = rest.astype(BF16)
        mix_ref[:, part * full : (part + 1) * full] = piece
        rest = rest - piece.astype(F32)


def up_kernel(count, *refs):
    block_refs = refs[:count]
    share_ref, gate_ref, up_ref, own_ref, send_ref, mix_ref = refs[count:]
    split_weights(share_ref, mix_ref)
    hidden = gate_ref.shape[1]
    rows = own_ref.shape[0]
    x = padded(join([b[...] for b in block_refs]))
    for low, high in tiles(x.shape[0], 256):
        for part, w_ref in enumerate((gate_ref, up_ref)):
            for at, size in tiles(hidden, 512):
                value = jnp.dot(
                    x[low : low + high], w_ref[:, at : at + size], preferred_element_type=F32
                )[: min(high, rows)]
                to = part * hidden + at
                own_ref[low : low + value.shape[0], to : to + size] = value
                send_ref[low : low + value.shape[0], to : to + size] = value.astype(BF16)


def down_kernel(own_ref, other_ref, down_ref, *block_refs):
    rows, hidden = own_ref.shape[0], down_ref.shape[0]
    total = own_ref[...] + other_ref[...].astype(F32)
    gate, up = total[:, :hidden], total[:, hidden:]
    act = padded((gate / (1.0 + jnp.exp(-gate)) * up).astype(BF16))
    for at, size in tiles(down_ref.shape[1], 512):
        value = jnp.dot(act, down_ref[:, at : at + size], preferred_element_type=F32)[:rows]
        spread(sorted_as(block_refs, RETURN, ORDER), value, at, size)


def mix_kernel(count, mix_ref, *refs):
    block_refs, (out_hbm, out_ref, sems) = refs[:count], refs[count:]
    mix = mix_ref[...]
    copies = []
    for i, (at, size) in enumerate(tiles(out_ref.shape[1], 512)):
        part = join(sorted_as([b[:, at : at + size] for b in block_refs], RETURN, ORDER))
        value = jnp.dot(
            mix, jnp.concatenate([part] * 3, axis=0), preferred_element_type=F32
        )
        out_ref[:, at : at + size] = value.astype(BF16)
        copy = pltpu.make_async_copy(
            out_ref.at[:, at : at + size], out_hbm.at[:, at : at + size], sems.at[i]
        )
        copy.start()
        copies.append(copy)
    for copy in copies:
        copy.wait()


def swap(blocks, order):
    return [
        lax.ppermute(block, "expert", [(i, i ^ j) for i in range(len(order))]) if j else block
        for block, j in zip(blocks, order)
    ]


def sorted_as(blocks, order, other):
    return [blocks[order.index(j)] for j in other] if len(blocks) > 1 else list(blocks)


def local(tokens, expert_ids, route_weight, gate_weight, up_weight, down_weight):
    devices = lax.axis_size("expert")
    split = HIDDEN_SIZE // gate_weight.shape[2]
    experts = devices // split
    count, width = tokens.shape
    top = expert_ids.shape[1]
    slots = min(max(4, 2 * count * top // ROUTED), count)
    hidden = gate_weight.shape[2]
    rows = devices * slots
    direct = split == 1 and devices == len(ORDER)
    near = functools.partial(pltpu.with_memory_space_constraint, memory_space=pltpu.VMEM)
    far = functools.partial(pltpu.with_memory_space_constraint, memory_space=pltpu.HBM)

    parts = devices if direct else 1
    sent = experts * slots // parts
    pick, share, held = pl.pallas_call(
        functools.partial(route_kernel, slots, split, direct),
        in_specs=[pl.BlockSpec(memory_space=pltpu.HBM)] * 3,
        out_specs=[VMEM] * 3,
        out_shape=[
            shape((experts * slots, count), BF16),
            shape((rows, count), F32),
            shape((count, width), BF16),
        ],
        scratch_shapes=[
            pltpu.VMEM((top, count), jnp.int32),
            pltpu.VMEM((top, count), F32),
            pltpu.SemaphoreType.DMA((3,)),
        ],
        compiler_params=params(tokens, shape((count, 8 * rows), F32)),
        cost_estimate=pl.CostEstimate(flops=int(1e6), bytes_accessed=0, transcendentals=0),
        name="route",
    )(far(expert_ids.T), far(route_weight.T), far(tokens))
    send = pl.pallas_call(
        send_kernel,
        in_specs=[VMEM] * 2,
        out_specs=[VMEM] * parts,
        out_shape=[shape((sent, width), BF16)] * parts,
        compiler_params=params(tokens, tokens),
        cost_estimate=pl.CostEstimate(flops=int(3e10), bytes_accessed=0, transcendentals=0),
        name="send",
    )(pick, held)
    if direct:
        arrived = swap(send, ORDER)
    else:
        spread_out = jnp.repeat(send[0].reshape(experts, slots, width), split, axis=0)
        arrived = [
            lax.all_to_all(spread_out, "expert", 0, 0, tiled=True).reshape(rows, width)
        ]

    own, give, mix = pl.pallas_call(
        functools.partial(up_kernel, parts),
        in_specs=[VMEM] * (parts + 3),
        out_specs=[VMEM] * 3,
        out_shape=[
            shape((rows, 2 * hidden), F32),
            shape((rows, 2 * hidden), BF16),
            shape((count, 3 * rows), BF16),
        ],
        compiler_params=params(shape((rows, width), F32), shape((rows, 2 * hidden), F32)),
        name="up",
    )(*arrived, share, near(gate_weight[0]), near(up_weight[0]))
    cores = lax.axis_size("tensor")
    other = lax.ppermute(give, "tensor", [(i, (i + 1) % cores) for i in range(cores)])
    answer = pl.pallas_call(
        down_kernel,
        in_specs=[VMEM] * 3,
        out_specs=[VMEM] * parts,
        out_shape=[shape((rows // parts, width), BF16)] * parts,
        compiler_params=params(shape((rows, 4 * hidden), F32), shape((rows, width), F32)),
        name="down",
    )(own, other, near(down_weight[0]))
    if direct:
        back = swap(answer, RETURN)
    else:
        back = [
            lax.all_to_all(
                answer[0].reshape(devices, slots, width), "expert", 0, 0, tiled=True
            ).reshape(rows, width)
        ]
    return pl.pallas_call(
        functools.partial(mix_kernel, parts),
        in_specs=[VMEM] * (1 + parts),
        out_specs=pl.BlockSpec(memory_space=pltpu.HBM),
        scratch_shapes=[
            pltpu.VMEM((count, width), BF16),
            pltpu.SemaphoreType.DMA((pl.cdiv(width, 512),)),
        ],
        out_shape=shape((count, width), BF16),
        compiler_params=params(mix, tokens, shape((rows, width), BF16)),
        name="mix",
    )(mix, *back)


def solution(mesh):
    return jax.shard_map(
        local,
        mesh=mesh,
        in_specs=(
            P(("groups", "expert"), "tensor"),
            P(("groups", "expert"), None),
            P(("groups", "expert"), None),
            P("expert", "tensor", None),
            P("expert", "tensor", None),
            P("expert", None, "tensor"),
        ),
        out_specs=P(("groups", "expert"), "tensor"),
        check_vma=False,
    )
```

```python
import functools

import jax
import jax.numpy as jnp
from jax import lax
from jax.experimental import pallas as pl
from jax.experimental.pallas import tpu as pltpu
from jax.sharding import PartitionSpec as P

HIDDEN_SIZE = 2048
ROUTED = 256
ORDER = (0, 7, 6, 5, 3, 4, 2, 1)
RETURN = (0, 5, 6, 3, 7, 2, 4, 1)
BF16 = jnp.bfloat16
F32 = jnp.float32
VMEM = pl.BlockSpec(memory_space=pltpu.VMEM)


def params(*arrays):
    size = sum(a.size * a.dtype.itemsize for a in arrays)
    return pltpu.CompilerParams(vmem_limit_bytes=int(1.25 * size) + (3 << 20))


def shape(dims, dtype):
    return jax.ShapeDtypeStruct(dims, dtype)


def tiles(total, size):
    return [(at, min(size, total - at)) for at in range(0, total, size)]


def join(blocks):
    if len(blocks) == 1:
        return blocks[0]
    return jnp.concatenate([b.astype(F32) for b in blocks], axis=0).astype(BF16)


def padded(x):
    short = 128 - x.shape[0]
    return x if short <= 0 else jnp.concatenate([x, jnp.zeros((short, x.shape[1]), x.dtype)], axis=0)


def partner(place):
    return sum(jnp.where(place == at, j, 0) for at, j in enumerate(ORDER) if j)


def spread(refs, value, at, size):
    rows = value.shape[0] // len(refs)
    for j, ref in enumerate(refs):
        ref[:, at : at + size] = value[j * rows : (j + 1) * rows].astype(BF16)


def route_kernel(
    slots, split, direct, ids_hbm, weight_hbm, tokens_hbm, pick_ref, share_ref, tokens_ref, *rest
):
    ids_ref, weight_ref, sems = rest
    top, tokens = ids_ref.shape
    full = share_ref.shape[0]
    rows = full // split
    copies = [
        pltpu.make_async_copy(ids_hbm, ids_ref, sems.at[0]),
        pltpu.make_async_copy(weight_hbm, weight_ref, sems.at[1]),
        pltpu.make_async_copy(tokens_hbm, tokens_ref, sems.at[2]),
    ]
    for copy in copies:
        copy.start()
    copies[0].wait()
    copies[1].wait()

    def named(count, per):
        expert = lax.broadcasted_iota(jnp.int32, (count, tokens), 0) // per
        if direct:
            expert = partner(expert) ^ lax.axis_index("expert")
        hit = jnp.zeros((count, tokens), F32)
        scale = jnp.zeros((count, tokens), F32)
        for k in range(top):
            same = ids_ref[k : k + 1, :] == expert
            hit = jnp.where(same, 1.0, hit)
            scale = jnp.where(same, weight_ref[k : k + 1, :], scale)
        earlier = lax.broadcasted_iota(jnp.int32, (tokens, tokens), 0) < lax.broadcasted_iota(
            jnp.int32, (tokens, tokens), 1
        )
        before = jnp.dot(
            hit.astype(BF16), earlier.astype(F32).astype(BF16), preferred_element_type=F32
        ).astype(jnp.int32)
        slot = lax.broadcasted_iota(jnp.int32, (count, tokens), 0) % slots
        return jnp.where(before == slot, hit, 0.0), scale

    chosen, scale = named(rows, slots)
    pick_ref[...] = chosen.astype(BF16)
    if split > 1:
        chosen, scale = named(full, slots * split)
    share_ref[...] = chosen * scale
    copies[2].wait()


def send_kernel(pick_ref, tokens_ref, *block_refs):
    pick = pick_ref[...]
    for at, size in tiles(tokens_ref.shape[1], 512):
        value = jnp.dot(pick, tokens_ref[:, at : at + size], preferred_element_type=F32)
        spread(block_refs, value, at, size)


def split_weights(share_ref, mix_ref):
    full = share_ref.shape[0]
    rest = share_ref[...].T
    for part in range(3):
        piece = rest.astype(BF16)
        mix_ref[:, part * full : (part + 1) * full] = piece
        rest = rest - piece.astype(F32)


def up_kernel(count, *refs):
    block_refs = refs[:count]
    share_ref, gate_ref, up_ref, own_ref, send_ref, mix_ref = refs[count:]
    split_weights(share_ref, mix_ref)
    hidden = gate_ref.shape[1]
    rows = own_ref.shape[0]
    x = padded(join([b[...] for b in block_refs]))
    for low, high in tiles(x.shape[0], 256):
        for part, w_ref in enumerate((gate_ref, up_ref)):
            for at, size in tiles(hidden, 512):
                value = jnp.dot(
                    x[low : low + high], w_ref[:, at : at + size], preferred_element_type=F32
                )[: min(high, rows)]
                to = part * hidden + at
                own_ref[low : low + value.shape[0], to : to + size] = value
                send_ref[low : low + value.shape[0], to : to + size] = value.astype(BF16)


def down_kernel(own_ref, other_ref, down_ref, *block_refs):
    rows, hidden = own_ref.shape[0], down_ref.shape[0]
    total = own_ref[...] + other_ref[...].astype(F32)
    gate, up = total[:, :hidden], total[:, hidden:]
    act = padded((gate / (1.0 + jnp.exp(-gate)) * up).astype(BF16))
    for at, size in tiles(down_ref.shape[1], 512):
        value = jnp.dot(act, down_ref[:, at : at + size], preferred_element_type=F32)[:rows]
        spread(sorted_as(block_refs, RETURN, ORDER), value, at, size)


def mix_kernel(count, mix_ref, *refs):
    block_refs, (out_hbm, out_ref, sems) = refs[:count], refs[count:]
    mix = mix_ref[...]
    copies = []
    for i, (at, size) in enumerate(tiles(out_ref.shape[1], 512)):
        part = join(sorted_as([b[:, at : at + size] for b in block_refs], RETURN, ORDER))
        value = jnp.dot(
            mix, jnp.concatenate([part] * 3, axis=0), preferred_element_type=F32
        )
        out_ref[:, at : at + size] = value.astype(BF16)
        copy = pltpu.make_async_copy(
            out_ref.at[:, at : at + size], out_hbm.at[:, at : at + size], sems.at[i]
        )
        copy.start()
        copies.append(copy)
    for copy in copies:
        copy.wait()


def swap(blocks, order):
    return [
        lax.ppermute(block, "expert", [(i, i ^ j) for i in range(len(order))]) if j else block
        for block, j in zip(blocks, order)
    ]


def sorted_as(blocks, order, other):
    return [blocks[order.index(j)] for j in other] if len(blocks) > 1 else list(blocks)


def local(tokens, expert_ids, route_weight, gate_weight, up_weight, down_weight):
    devices = lax.axis_size("expert")
    split = HIDDEN_SIZE // gate_weight.shape[2]
    experts = devices // split
    count, width = tokens.shape
    top = expert_ids.shape[1]
    slots = min(max(4, 2 * count * top // ROUTED), count)
    hidden = gate_weight.shape[2]
    rows = devices * slots
    direct = split == 1 and devices == len(ORDER)
    near = functools.partial(pltpu.with_memory_space_constraint, memory_space=pltpu.VMEM)
    far = functools.partial(pltpu.with_memory_space_constraint, memory_space=pltpu.HBM)

    parts = devices if direct else 1
    sent = experts * slots // parts
    pick, share, held = pl.pallas_call(
        functools.partial(route_kernel, slots, split, direct),
        in_specs=[pl.BlockSpec(memory_space=pltpu.HBM)] * 3,
        out_specs=[VMEM] * 3,
        out_shape=[
            shape((experts * slots, count), BF16),
            shape((rows, count), F32),
            shape((count, width), BF16),
        ],
        scratch_shapes=[
            pltpu.VMEM((top, count), jnp.int32),
            pltpu.VMEM((top, count), F32),
            pltpu.SemaphoreType.DMA((3,)),
        ],
        compiler_params=params(tokens, shape((count, 8 * rows), F32)),
        cost_estimate=pl.CostEstimate(flops=int(1e6), bytes_accessed=0, transcendentals=0),
        name="route",
    )(far(expert_ids.T), far(route_weight.T), far(tokens))
    send = pl.pallas_call(
        send_kernel,
        in_specs=[VMEM] * 2,
        out_specs=[VMEM] * parts,
        out_shape=[shape((sent, width), BF16)] * parts,
        compiler_params=params(tokens, tokens),
        cost_estimate=pl.CostEstimate(flops=int(3e10), bytes_accessed=0, transcendentals=0),
        name="send",
    )(pick, held)
    if direct:
        arrived = swap(send, ORDER)
    else:
        spread_out = jnp.repeat(send[0].reshape(experts, slots, width), split, axis=0)
        arrived = [
            lax.all_to_all(spread_out, "expert", 0, 0, tiled=True).reshape(rows, width)
        ]

    own, give, mix = pl.pallas_call(
        functools.partial(up_kernel, parts),
        in_specs=[VMEM] * (parts + 3),
        out_specs=[VMEM] * 3,
        out_shape=[
            shape((rows, 2 * hidden), F32),
            shape((rows, 2 * hidden), BF16),
            shape((count, 3 * rows), BF16),
        ],
        compiler_params=params(shape((rows, width), F32), shape((rows, 2 * hidden), F32)),
        name="up",
    )(*arrived, share, near(gate_weight[0]), near(up_weight[0]))
    cores = lax.axis_size("tensor")
    other = lax.ppermute(give, "tensor", [(i, (i + 1) % cores) for i in range(cores)])
    answer = pl.pallas_call(
        down_kernel,
        in_specs=[VMEM] * 3,
        out_specs=[VMEM] * parts,
        out_shape=[shape((rows // parts, width), BF16)] * parts,
        compiler_params=params(shape((rows, 4 * hidden), F32), shape((rows, width), F32)),
        name="down",
    )(own, other, near(down_weight[0]))
    if direct:
        back = swap(answer, RETURN)
    else:
        back = [
            lax.all_to_all(
                answer[0].reshape(devices, slots, width), "expert", 0, 0, tiled=True
            ).reshape(rows, width)
        ]
    return pl.pallas_call(
        functools.partial(mix_kernel, parts),
        in_specs=[VMEM] * (1 + parts),
        out_specs=pl.BlockSpec(memory_space=pltpu.HBM),
        scratch_shapes=[
            pltpu.VMEM((count, width), BF16),
            pltpu.SemaphoreType.DMA((pl.cdiv(width, 512),)),
        ],
        out_shape=shape((count, width), BF16),
        compiler_params=params(mix, tokens, shape((rows, width), BF16)),
        name="mix",
    )(mix, *back)


def solution(mesh):
    return jax.shard_map(
        local,
        mesh=mesh,
        in_specs=(
            P(("groups", "expert"), "tensor"),
            P(("groups", "expert"), None),
            P(("groups", "expert"), None),
            P("expert", "tensor", None),
            P("expert", "tensor", None),
            P("expert", None, "tensor"),
        ),
        out_specs=P(("groups", "expert"), "tensor"),
        check_vma=False,
    )
```

```python
import functools

import jax
import jax.numpy as jnp
from jax import lax
from jax.experimental import pallas as pl
from jax.experimental.pallas import tpu as pltpu
from jax.sharding import PartitionSpec as P

HIDDEN_SIZE = 2048
ROUTED = 256
ORDER = (0, 7, 6, 5, 3, 4, 2, 1)
RETURN = (0, 5, 6, 7, 3, 4, 2, 1)
BF16 = jnp.bfloat16
F32 = jnp.float32
VMEM = pl.BlockSpec(memory_space=pltpu.VMEM)


def params(*arrays):
    size = sum(a.size * a.dtype.itemsize for a in arrays)
    return pltpu.CompilerParams(vmem_limit_bytes=int(1.25 * size) + (3 << 20))


def shape(dims, dtype):
    return jax.ShapeDtypeStruct(dims, dtype)


def tiles(total, size):
    return [(at, min(size, total - at)) for at in range(0, total, size)]


def join(blocks):
    if len(blocks) == 1:
        return blocks[0]
    return jnp.concatenate([b.astype(F32) for b in blocks], axis=0).astype(BF16)


def padded(x):
    short = 128 - x.shape[0]
    return x if short <= 0 else jnp.concatenate([x, jnp.zeros((short, x.shape[1]), x.dtype)], axis=0)


def partner(place):
    return sum(jnp.where(place == at, j, 0) for at, j in enumerate(ORDER) if j)


def spread(refs, value, at, size):
    rows = value.shape[0] // len(refs)
    for j, ref in enumerate(refs):
        ref[:, at : at + size] = value[j * rows : (j + 1) * rows].astype(BF16)


def route_kernel(
    slots, split, direct, ids_hbm, weight_hbm, tokens_hbm, pick_ref, share_ref, tokens_ref, *rest
):
    ids_ref, weight_ref, sems = rest
    top, tokens = ids_ref.shape
    full = share_ref.shape[0]
    rows = full // split
    copies = [
        pltpu.make_async_copy(ids_hbm, ids_ref, sems.at[0]),
        pltpu.make_async_copy(weight_hbm, weight_ref, sems.at[1]),
        pltpu.make_async_copy(tokens_hbm, tokens_ref, sems.at[2]),
    ]
    for copy in copies:
        copy.start()
    copies[0].wait()
    copies[1].wait()

    def named(count, per):
        expert = lax.broadcasted_iota(jnp.int32, (count, tokens), 0) // per
        if direct:
            expert = partner(expert) ^ lax.axis_index("expert")
        hit = jnp.zeros((count, tokens), F32)
        scale = jnp.zeros((count, tokens), F32)
        for k in range(top):
            same = ids_ref[k : k + 1, :] == expert
            hit = jnp.where(same, 1.0, hit)
            scale = jnp.where(same, weight_ref[k : k + 1, :], scale)
        earlier = lax.broadcasted_iota(jnp.int32, (tokens, tokens), 0) < lax.broadcasted_iota(
            jnp.int32, (tokens, tokens), 1
        )
        before = jnp.dot(
            hit.astype(BF16), earlier.astype(F32).astype(BF16), preferred_element_type=F32
        ).astype(jnp.int32)
        slot = lax.broadcasted_iota(jnp.int32, (count, tokens), 0) % slots
        return jnp.where(before == slot, hit, 0.0), scale

    chosen, scale = named(rows, slots)
    pick_ref[...] = chosen.astype(BF16)
    if split > 1:
        chosen, scale = named(full, slots * split)
    share_ref[...] = chosen * scale
    copies[2].wait()


def send_kernel(pick_ref, tokens_ref, *block_refs):
    pick = pick_ref[...]
    for at, size in tiles(tokens_ref.shape[1], 512):
        value = jnp.dot(pick, tokens_ref[:, at : at + size], preferred_element_type=F32)
        spread(block_refs, value, at, size)


def split_weights(share_ref, mix_ref):
    full = share_ref.shape[0]
    rest = share_ref[...].T
    for part in range(3):
        piece = rest.astype(BF16)
        mix_ref[:, part * full : (part + 1) * full] = piece
        rest = rest - piece.astype(F32)


def up_kernel(count, *refs):
    block_refs = refs[:count]
    share_ref, gate_ref, up_ref, own_ref, send_ref, mix_ref = refs[count:]
    split_weights(share_ref, mix_ref)
    hidden = gate_ref.shape[1]
    rows = own_ref.shape[0]
    x = padded(join([b[...] for b in block_refs]))
    for low, high in tiles(x.shape[0], 256):
        for part, w_ref in enumerate((gate_ref, up_ref)):
            for at, size in tiles(hidden, 512):
                value = jnp.dot(
                    x[low : low + high], w_ref[:, at : at + size], preferred_element_type=F32
                )[: min(high, rows)]
                to = part * hidden + at
                own_ref[low : low + value.shape[0], to : to + size] = value
                send_ref[low : low + value.shape[0], to : to + size] = value.astype(BF16)


def down_kernel(own_ref, other_ref, down_ref, *block_refs):
    rows, hidden = own_ref.shape[0], down_ref.shape[0]
    total = own_ref[...] + other_ref[...].astype(F32)
    gate, up = total[:, :hidden], total[:, hidden:]
    act = padded((gate / (1.0 + jnp.exp(-gate)) * up).astype(BF16))
    for at, size in tiles(down_ref.shape[1], 512):
        value = jnp.dot(act, down_ref[:, at : at + size], preferred_element_type=F32)[:rows]
        spread(sorted_as(block_refs, RETURN, ORDER), value, at, size)


def mix_kernel(count, mix_ref, *refs):
    block_refs, (out_hbm, out_ref, sems) = refs[:count], refs[count:]
    mix = mix_ref[...]
    copies = []
    for i, (at, size) in enumerate(tiles(out_ref.shape[1], 512)):
        part = join(sorted_as([b[:, at : at + size] for b in block_refs], RETURN, ORDER))
        value = jnp.dot(
            mix, jnp.concatenate([part] * 3, axis=0), preferred_element_type=F32
        )
        out_ref[:, at : at + size] = value.astype(BF16)
        copy = pltpu.make_async_copy(
            out_ref.at[:, at : at + size], out_hbm.at[:, at : at + size], sems.at[i]
        )
        copy.start()
        copies.append(copy)
    for copy in copies:
        copy.wait()


def swap(blocks, order):
    return [
        lax.ppermute(block, "expert", [(i, i ^ j) for i in range(len(order))]) if j else block
        for block, j in zip(blocks, order)
    ]


def sorted_as(blocks, order, other):
    return [blocks[order.index(j)] for j in other] if len(blocks) > 1 else list(blocks)


def local(tokens, expert_ids, route_weight, gate_weight, up_weight, down_weight):
    devices = lax.axis_size("expert")
    split = HIDDEN_SIZE // gate_weight.shape[2]
    experts = devices // split
    count, width = tokens.shape
    top = expert_ids.shape[1]
    slots = min(max(4, 2 * count * top // ROUTED), count)
    hidden = gate_weight.shape[2]
    rows = devices * slots
    direct = split == 1 and devices == len(ORDER)
    near = functools.partial(pltpu.with_memory_space_constraint, memory_space=pltpu.VMEM)
    far = functools.partial(pltpu.with_memory_space_constraint, memory_space=pltpu.HBM)

    parts = devices if direct else 1
    sent = experts * slots // parts
    pick, share, held = pl.pallas_call(
        functools.partial(route_kernel, slots, split, direct),
        in_specs=[pl.BlockSpec(memory_space=pltpu.HBM)] * 3,
        out_specs=[VMEM] * 3,
        out_shape=[
            shape((experts * slots, count), BF16),
            shape((rows, count), F32),
            shape((count, width), BF16),
        ],
        scratch_shapes=[
            pltpu.VMEM((top, count), jnp.int32),
            pltpu.VMEM((top, count), F32),
            pltpu.SemaphoreType.DMA((3,)),
        ],
        compiler_params=params(tokens, shape((count, 8 * rows), F32)),
        cost_estimate=pl.CostEstimate(flops=int(1e6), bytes_accessed=0, transcendentals=0),
        name="route",
    )(far(expert_ids.T), far(route_weight.T), far(tokens))
    send = pl.pallas_call(
        send_kernel,
        in_specs=[VMEM] * 2,
        out_specs=[VMEM] * parts,
        out_shape=[shape((sent, width), BF16)] * parts,
        compiler_params=params(tokens, tokens),
        cost_estimate=pl.CostEstimate(flops=int(3e10), bytes_accessed=0, transcendentals=0),
        name="send",
    )(pick, held)
    if direct:
        arrived = swap(send, ORDER)
    else:
        spread_out = jnp.repeat(send[0].reshape(experts, slots, width), split, axis=0)
        arrived = [
            lax.all_to_all(spread_out, "expert", 0, 0, tiled=True).reshape(rows, width)
        ]

    own, give, mix = pl.pallas_call(
        functools.partial(up_kernel, parts),
        in_specs=[VMEM] * (parts + 3),
        out_specs=[VMEM] * 3,
        out_shape=[
            shape((rows, 2 * hidden), F32),
            shape((rows, 2 * hidden), BF16),
            shape((count, 3 * rows), BF16),
        ],
        compiler_params=params(shape((rows, width), F32), shape((rows, 2 * hidden), F32)),
        name="up",
    )(*arrived, share, near(gate_weight[0]), near(up_weight[0]))
    cores = lax.axis_size("tensor")
    other = lax.ppermute(give, "tensor", [(i, (i + 1) % cores) for i in range(cores)])
    answer = pl.pallas_call(
        down_kernel,
        in_specs=[VMEM] * 3,
        out_specs=[VMEM] * parts,
        out_shape=[shape((rows // parts, width), BF16)] * parts,
        compiler_params=params(shape((rows, 4 * hidden), F32), shape((rows, width), F32)),
        name="down",
    )(own, other, near(down_weight[0]))
    if direct:
        back = swap(answer, RETURN)
    else:
        back = [
            lax.all_to_all(
                answer[0].reshape(devices, slots, width), "expert", 0, 0, tiled=True
            ).reshape(rows, width)
        ]
    return pl.pallas_call(
        functools.partial(mix_kernel, parts),
        in_specs=[VMEM] * (1 + parts),
        out_specs=pl.BlockSpec(memory_space=pltpu.HBM),
        scratch_shapes=[
            pltpu.VMEM((count, width), BF16),
            pltpu.SemaphoreType.DMA((pl.cdiv(width, 512),)),
        ],
        out_shape=shape((count, width), BF16),
        compiler_params=params(mix, tokens, shape((rows, width), BF16)),
        name="mix",
    )(mix, *back)


def solution(mesh):
    return jax.shard_map(
        local,
        mesh=mesh,
        in_specs=(
            P(("groups", "expert"), "tensor"),
            P(("groups", "expert"), None),
            P(("groups", "expert"), None),
            P("expert", "tensor", None),
            P("expert", "tensor", None),
            P("expert", None, "tensor"),
        ),
        out_specs=P(("groups", "expert"), "tensor"),
        check_vma=False,
    )
```

```python
import functools

import jax
import jax.numpy as jnp
from jax import lax
from jax.experimental import pallas as pl
from jax.experimental.pallas import tpu as pltpu
from jax.sharding import PartitionSpec as P

HIDDEN_SIZE = 2048
ROUTED = 256
ORDER = (0, 7, 6, 3, 5, 4, 2, 1)
RETURN = (0, 5, 6, 3, 7, 2, 4, 1)
BF16 = jnp.bfloat16
F32 = jnp.float32
VMEM = pl.BlockSpec(memory_space=pltpu.VMEM)


def params(*arrays):
    size = sum(a.size * a.dtype.itemsize for a in arrays)
    return pltpu.CompilerParams(vmem_limit_bytes=int(1.25 * size) + (3 << 20))


def shape(dims, dtype):
    return jax.ShapeDtypeStruct(dims, dtype)


def tiles(total, size):
    return [(at, min(size, total - at)) for at in range(0, total, size)]


def join(blocks):
    if len(blocks) == 1:
        return blocks[0]
    return jnp.concatenate([b.astype(F32) for b in blocks], axis=0).astype(BF16)


def padded(x):
    short = 128 - x.shape[0]
    return x if short <= 0 else jnp.concatenate([x, jnp.zeros((short, x.shape[1]), x.dtype)], axis=0)


def partner(place):
    return sum(jnp.where(place == at, j, 0) for at, j in enumerate(ORDER) if j)


def spread(refs, value, at, size):
    rows = value.shape[0] // len(refs)
    for j, ref in enumerate(refs):
        ref[:, at : at + size] = value[j * rows : (j + 1) * rows].astype(BF16)


def route_kernel(
    slots, split, direct, ids_hbm, weight_hbm, tokens_hbm, pick_ref, share_ref, tokens_ref, *rest
):
    ids_ref, weight_ref, sems = rest
    top, tokens = ids_ref.shape
    full = share_ref.shape[0]
    rows = full // split
    copies = [
        pltpu.make_async_copy(ids_hbm, ids_ref, sems.at[0]),
        pltpu.make_async_copy(weight_hbm, weight_ref, sems.at[1]),
        pltpu.make_async_copy(tokens_hbm, tokens_ref, sems.at[2]),
    ]
    for copy in copies:
        copy.start()
    copies[0].wait()
    copies[1].wait()

    def named(count, per):
        expert = lax.broadcasted_iota(jnp.int32, (count, tokens), 0) // per
        if direct:
            expert = partner(expert) ^ lax.axis_index("expert")
        hit = jnp.zeros((count, tokens), F32)
        scale = jnp.zeros((count, tokens), F32)
        for k in range(top):
            same = ids_ref[k : k + 1, :] == expert
            hit = jnp.where(same, 1.0, hit)
            scale = jnp.where(same, weight_ref[k : k + 1, :], scale)
        earlier = lax.broadcasted_iota(jnp.int32, (tokens, tokens), 0) < lax.broadcasted_iota(
            jnp.int32, (tokens, tokens), 1
        )
        before = jnp.dot(
            hit.astype(BF16), earlier.astype(F32).astype(BF16), preferred_element_type=F32
        ).astype(jnp.int32)
        slot = lax.broadcasted_iota(jnp.int32, (count, tokens), 0) % slots
        return jnp.where(before == slot, hit, 0.0), scale

    chosen, scale = named(rows, slots)
    pick_ref[...] = chosen.astype(BF16)
    if split > 1:
        chosen, scale = named(full, slots * split)
    share_ref[...] = chosen * scale
    copies[2].wait()


def send_kernel(pick_ref, tokens_ref, *block_refs):
    pick = pick_ref[...]
    for at, size in tiles(tokens_ref.shape[1], 512):
        value = jnp.dot(pick, tokens_ref[:, at : at + size], preferred_element_type=F32)
        spread(block_refs, value, at, size)


def split_weights(share_ref, mix_ref):
    full = share_ref.shape[0]
    rest = share_ref[...].T
    for part in range(3):
        piece = rest.astype(BF16)
        mix_ref[:, part * full : (part + 1) * full] = piece
        rest = rest - piece.astype(F32)


def up_kernel(count, *refs):
    block_refs = refs[:count]
    share_ref, gate_ref, up_ref, own_ref, send_ref, mix_ref = refs[count:]
    split_weights(share_ref, mix_ref)
    hidden = gate_ref.shape[1]
    rows = own_ref.shape[0]
    x = padded(join([b[...] for b in block_refs]))
    for low, high in tiles(x.shape[0], 256):
        for part, w_ref in enumerate((gate_ref, up_ref)):
            for at, size in tiles(hidden, 512):
                value = jnp.dot(
                    x[low : low + high], w_ref[:, at : at + size], preferred_element_type=F32
                )[: min(high, rows)]
                to = part * hidden + at
                own_ref[low : low + value.shape[0], to : to + size] = value
                send_ref[low : low + value.shape[0], to : to + size] = value.astype(BF16)


def down_kernel(own_ref, other_ref, down_ref, *block_refs):
    rows, hidden = own_ref.shape[0], down_ref.shape[0]
    total = own_ref[...] + other_ref[...].astype(F32)
    gate, up = total[:, :hidden], total[:, hidden:]
    act = padded((gate / (1.0 + jnp.exp(-gate)) * up).astype(BF16))
    for at, size in tiles(down_ref.shape[1], 512):
        value = jnp.dot(act, down_ref[:, at : at + size], preferred_element_type=F32)[:rows]
        spread(sorted_as(block_refs, RETURN, ORDER), value, at, size)


def mix_kernel(count, mix_ref, *refs):
    block_refs, (out_hbm, out_ref, sems) = refs[:count], refs[count:]
    mix = mix_ref[...]
    copies = []
    for i, (at, size) in enumerate(tiles(out_ref.shape[1], 512)):
        part = join(sorted_as([b[:, at : at + size] for b in block_refs], RETURN, ORDER))
        value = jnp.dot(
            mix, jnp.concatenate([part] * 3, axis=0), preferred_element_type=F32
        )
        out_ref[:, at : at + size] = value.astype(BF16)
        copy = pltpu.make_async_copy(
            out_ref.at[:, at : at + size], out_hbm.at[:, at : at + size], sems.at[i]
        )
        copy.start()
        copies.append(copy)
    for copy in copies:
        copy.wait()


def swap(blocks, order):
    return [
        lax.ppermute(block, "expert", [(i, i ^ j) for i in range(len(order))]) if j else block
        for block, j in zip(blocks, order)
    ]


def sorted_as(blocks, order, other):
    return [blocks[order.index(j)] for j in other] if len(blocks) > 1 else list(blocks)


def local(tokens, expert_ids, route_weight, gate_weight, up_weight, down_weight):
    devices = lax.axis_size("expert")
    split = HIDDEN_SIZE // gate_weight.shape[2]
    experts = devices // split
    count, width = tokens.shape
    top = expert_ids.shape[1]
    slots = min(max(4, 2 * count * top // ROUTED), count)
    hidden = gate_weight.shape[2]
    rows = devices * slots
    direct = split == 1 and devices == len(ORDER)
    near = functools.partial(pltpu.with_memory_space_constraint, memory_space=pltpu.VMEM)
    far = functools.partial(pltpu.with_memory_space_constraint, memory_space=pltpu.HBM)

    parts = devices if direct else 1
    sent = experts * slots // parts
    pick, share, held = pl.pallas_call(
        functools.partial(route_kernel, slots, split, direct),
        in_specs=[pl.BlockSpec(memory_space=pltpu.HBM)] * 3,
        out_specs=[VMEM] * 3,
        out_shape=[
            shape((experts * slots, count), BF16),
            shape((rows, count), F32),
            shape((count, width), BF16),
        ],
        scratch_shapes=[
            pltpu.VMEM((top, count), jnp.int32),
            pltpu.VMEM((top, count), F32),
            pltpu.SemaphoreType.DMA((3,)),
        ],
        compiler_params=params(tokens, shape((count, 8 * rows), F32)),
        cost_estimate=pl.CostEstimate(flops=int(1e6), bytes_accessed=0, transcendentals=0),
        name="route",
    )(far(expert_ids.T), far(route_weight.T), far(tokens))
    send = pl.pallas_call(
        send_kernel,
        in_specs=[VMEM] * 2,
        out_specs=[VMEM] * parts,
        out_shape=[shape((sent, width), BF16)] * parts,
        compiler_params=params(tokens, tokens),
        cost_estimate=pl.CostEstimate(flops=int(3e10), bytes_accessed=0, transcendentals=0),
        name="send",
    )(pick, held)
    if direct:
        arrived = swap(send, ORDER)
    else:
        spread_out = jnp.repeat(send[0].reshape(experts, slots, width), split, axis=0)
        arrived = [
            lax.all_to_all(spread_out, "expert", 0, 0, tiled=True).reshape(rows, width)
        ]

    own, give, mix = pl.pallas_call(
        functools.partial(up_kernel, parts),
        in_specs=[VMEM] * (parts + 3),
        out_specs=[VMEM] * 3,
        out_shape=[
            shape((rows, 2 * hidden), F32),
            shape((rows, 2 * hidden), BF16),
            shape((count, 3 * rows), BF16),
        ],
        compiler_params=params(shape((rows, width), F32), shape((rows, 2 * hidden), F32)),
        name="up",
    )(*arrived, share, near(gate_weight[0]), near(up_weight[0]))
    cores = lax.axis_size("tensor")
    other = lax.ppermute(give, "tensor", [(i, (i + 1) % cores) for i in range(cores)])
    answer = pl.pallas_call(
        down_kernel,
        in_specs=[VMEM] * 3,
        out_specs=[VMEM] * parts,
        out_shape=[shape((rows // parts, width), BF16)] * parts,
        compiler_params=params(shape((rows, 4 * hidden), F32), shape((rows, width), F32)),
        name="down",
    )(own, other, near(down_weight[0]))
    if direct:
        back = swap(answer, RETURN)
    else:
        back = [
            lax.all_to_all(
                answer[0].reshape(devices, slots, width), "expert", 0, 0, tiled=True
            ).reshape(rows, width)
        ]
    return pl.pallas_call(
        functools.partial(mix_kernel, parts),
        in_specs=[VMEM] * (1 + parts),
        out_specs=pl.BlockSpec(memory_space=pltpu.HBM),
        scratch_shapes=[
            pltpu.VMEM((count, width), BF16),
            pltpu.SemaphoreType.DMA((pl.cdiv(width, 512),)),
        ],
        out_shape=shape((count, width), BF16),
        compiler_params=params(mix, tokens, shape((rows, width), BF16)),
        name="mix",
    )(mix, *back)


def solution(mesh):
    return jax.shard_map(
        local,
        mesh=mesh,
        in_specs=(
            P(("groups", "expert"), "tensor"),
            P(("groups", "expert"), None),
            P(("groups", "expert"), None),
            P("expert", "tensor", None),
            P("expert", "tensor", None),
            P("expert", None, "tensor"),
        ),
        out_specs=P(("groups", "expert"), "tensor"),
        check_vma=False,
    )
```
